32 devices in a mesh: groups: 2 (over x), store: 8 (over z, y), tensor: 2 (over core).
Axes of the slice: x: 2, y: 2, z: 4, core: 2. Of those that a mesh axis runs over, the one named last changes fastest.
Arguments:
- hidden_in: bfloat16 [6144, 8192], P(('groups', 'store'), 'tensor'), parts along dimension 0, may hold values from -6 to 6
- base_weight: bfloat16 [8192, 1024], P('tensor'), may hold values from -0.0625 to 0.0625
- adapter_down: bfloat16 [32, 8192, 64], P(('groups', 'store'), 'tensor'), parts along dimension 0, may hold values from -0.0625 to 0.0625
- adapter_up: bfloat16 [32, 64, 1024], P(('groups', 'store')), parts along dimension 0, may hold values from -0.75 to 0.75
- lengths: int32 [768], P(('groups', 'store')), parts along dimension 0, may hold values from 1 to 15, as said below
- adapter_ids: int32 [768], P(('groups', 'store')), parts along dimension 0, may hold values from 0 to 15, as said below
Outputs:
- key_proj: bfloat16 [6144, 1024], P(('groups', 'store'), 'tensor'), parts along dimension 0
The draws below stay inside these ranges and needn't reach their ends.
There are 2 independent parts, one for each index of `groups`. The reference program is written for one: setup_inputs(seed, part) draws one part's arguments, and reference() takes and returns one part's arrays. A program takes and returns all parts, laid end to end along the dimension named above; an argument that names none is the same for every part. Nothing has to cross between parts.
Inputs may be any that keep to these rules, and one draw needn't show every extreme that they name: The lengths of the requests of one store index sum to 384. The owner of adapter a is store index a // 2; the requests of one store index send at most 90 tokens to the adapters of one owner, and some owner gets exactly 90 from every store index. `adapter_ids`: adapter of each request, owned as stated for lengths.
All inputs are finite; a program needn't handle non-finite values.
Results may differ from the reference program's by a relative error of at most 0.012.
Values may be sent and summed in bfloat16 or wider, within the bound.
A program may use at most 128 MiB of HBM per device.

```python
import jax
import jax.numpy as jnp
from jax import lax

D = 8192
KEY_FEATURES = 1024
RANK = 64
TOK_DEV = 384
LONGEST_LENGTH = 15
ADP_DEV = 2
REQUESTS_PER_STORE = 48
TOKENS = 3072
ADAPTERS = 16
N_STORE = 8


def make_plan(key):
    keys = jax.random.split(key, 5)
    popular_ordering = jax.random.permutation(keys[0], N_STORE)
    extra_credit = jnp.zeros((N_STORE,), jnp.int32).at[popular_ordering[:8]].set(1024)
    extra_credit = extra_credit.at[popular_ordering[0]].set(4096)
    random_jitter = jax.random.randint(keys[1], (N_STORE, N_STORE), 0, 1024)
    ranking_scores = (random_jitter + extra_credit[None, :]) * N_STORE + jnp.arange(N_STORE, dtype=jnp.int32)[None, :]
    unused, ranked = lax.top_k(ranking_scores, N_STORE)
    anchor = jax.random.randint(keys[2], (N_STORE, 1), 0, min(REQUESTS_PER_STORE, N_STORE))
    positions = jnp.arange(REQUESTS_PER_STORE, dtype=jnp.int32)[None, :]
    classes = (positions - anchor) % N_STORE
    owners = jnp.take_along_axis(ranked, classes, axis=1)
    first_half = jax.random.randint(keys[3], (N_STORE, REQUESTS_PER_STORE // 2), 1, LONGEST_LENGTH + 1)
    raw = jnp.stack([first_half, LONGEST_LENGTH + 1 - first_half], axis=2).reshape(N_STORE, REQUESTS_PER_STORE)
    forced = classes == 0
    partner = (jnp.bitwise_xor(positions, 1) - anchor) % N_STORE == 0
    span = jnp.where(forced, LONGEST_LENGTH, jnp.where(partner, 1, raw))
    local_pick = jax.random.randint(keys[4], (N_STORE, REQUESTS_PER_STORE), 0, ADP_DEV)
    chosen = owners * ADP_DEV + local_pick
    return (span.reshape(-1).astype(jnp.int32), chosen.reshape(-1).astype(jnp.int32))


def draw_lengths(key, part):
    span, chosen = make_plan(key)
    return span


def draw_adapter_ids(key, part):
    span, chosen = make_plan(key)
    return chosen


def steps_of(own_key, shape, cuts, smallest, high):
    level = 1.0
    for axis_at, parts in cuts:
        draws = jax.random.uniform(jax.random.fold_in(jax.random.fold_in(own_key, 6), axis_at), (parts,), jnp.float32, smallest / len(cuts), high / len(cuts))
        level = level * jnp.repeat(jnp.exp(draws), shape[axis_at] // parts).reshape((-1,) + (1,) * (len(shape) - 1 - axis_at))
    return level


def gaussian(rng, dims, scale, reach, cuts=(), held_as=jnp.bfloat16):
    result = scale * jax.random.normal(rng, dims, jnp.float32)
    if cuts:
        result = result * steps_of(rng, dims, cuts, -0.22, 0.18)
    return jnp.clip(result, -reach, reach).astype(held_as)


def setup_inputs(seed: int = 0, part: int = 0) -> dict:
    arg_keys = jax.random.split(jax.random.key(seed), 7)
    own_keys = jax.random.split(jax.random.fold_in(arg_keys[6], part), 7)
    return {
        "hidden_in": gaussian(own_keys[0], (TOKENS, D), 1.0, 6.0, ((0, 8), (1, 2))),
        "base_weight": gaussian(arg_keys[1], (D, KEY_FEATURES), D ** -0.5, 0.0625, ((0, 2),)),
        "adapter_down": gaussian(own_keys[2], (ADAPTERS, D, RANK), D ** -0.5, 0.0625, ((0, 8), (1, 2))),
        "adapter_up": gaussian(own_keys[3], (ADAPTERS, RANK, KEY_FEATURES), RANK ** -0.5, 0.75, ((0, 8),)),
        "lengths": draw_lengths(jax.random.fold_in(jax.random.fold_in(arg_keys[6], part), 71), part),
        "adapter_ids": draw_adapter_ids(jax.random.fold_in(jax.random.fold_in(arg_keys[6], part), 71), part),
    }


adapter_scale = 0.5


def reference(hidden_in, base_weight, adapter_down, adapter_up, lengths, adapter_ids):
    length_grid = lengths.reshape(N_STORE, REQUESTS_PER_STORE)
    id_grid = adapter_ids.reshape(N_STORE, REQUESTS_PER_STORE)
    request_ends = jnp.cumsum(length_grid, axis=1).astype(jnp.int32)
    request_starts = (request_ends - length_grid).astype(jnp.int32)
    inputs_grid = hidden_in.reshape(N_STORE, TOK_DEV, D)
    slot_steps = jnp.arange(LONGEST_LENGTH, dtype=jnp.int32)
    token_index = jnp.arange(TOK_DEV, dtype=jnp.int32)

    def one_index(packed):
        inputs, span, starts, ends, chosen_ids = packed
        row_index = starts[:, None] + slot_steps[None, :]
        valid = slot_steps[None, :] < span[:, None]
        row_index = jnp.where(valid, row_index, 0).astype(jnp.int32)
        gathered = inputs[row_index].astype(jnp.float32) * valid[..., None].astype(jnp.float32)
        down_mats = adapter_down[chosen_ids].astype(jnp.float32)
        shrink = jnp.einsum("qld,qdr->qlr", gathered, down_mats)
        up_mats = adapter_up[chosen_ids].astype(jnp.float32)
        broadcast_rows = jnp.einsum("qlr,qrk->qlk", shrink, up_mats, precision=lax.Precision.HIGHEST)
        broadcast_rows = lax.optimization_barrier(broadcast_rows.astype(jnp.bfloat16))
        request_lookup = jnp.sum((ends[None, :] <= token_index[:, None]).astype(jnp.int32), axis=1).astype(jnp.int32)
        start_shift = (token_index - starts[request_lookup]).astype(jnp.int32)
        adapter_token_rows = broadcast_rows.reshape(REQUESTS_PER_STORE * LONGEST_LENGTH, KEY_FEATURES)[(request_lookup * LONGEST_LENGTH + start_shift).astype(jnp.int32)]
        base_projection = jnp.dot(inputs, base_weight, preferred_element_type=jnp.float32)
        return (base_projection + adapter_scale * adapter_token_rows.astype(jnp.float32)).astype(jnp.bfloat16)

    results = lax.map(one_index, (inputs_grid, length_grid, request_starts, request_ends, id_grid))
    return results.reshape(N_STORE * TOK_DEV, KEY_FEATURES)
```

```python
import functools

import jax
import jax.numpy as jnp
from jax import lax
from jax.experimental import pallas as pl
from jax.experimental.pallas import tpu as pltpu
from jax.sharding import PartitionSpec as P

ADAPTER_SCALE = 0.5
MESH = pl.DeviceIdType.MESH
F32 = jnp.float32
BF16 = jnp.bfloat16


def adapter_of_token(lengths_row, ids_row, tokens):
    count = lengths_row.shape[1]
    down = lax.broadcasted_iota(jnp.int32, (count, count), 0)
    across = lax.broadcasted_iota(jnp.int32, (count, count), 1)
    column = jnp.sum(jnp.where(down == across, lengths_row, 0.0), axis=1, keepdims=True)
    ends = jnp.sum(jnp.where(down <= across, column, 0.0), axis=0, keepdims=True)
    starts = ends - lengths_row
    token = lax.broadcasted_iota(jnp.int32, (tokens, count), 0).astype(F32)
    inside = (token >= starts) & (token < ends)
    return jnp.sum(jnp.where(inside, ids_row, 0.0), axis=1, keepdims=True)


def kernel(
    n, x_ref, w_ref, down_ref, up_ref, len_ref, ids_ref, out_ref,
    xv, x2, wb, dv, uv, stage, big, upx, meta, metap, tok, acc, snd, rcv,
    basev, bsend, brecv,
    loc, wsem, ls, lr, pair_s, pair_r, us, ur, ss, sr,
):
    tokens = x_ref.shape[0]
    quarter = x_ref.shape[1] // 2
    adapters, _, rank = down_ref.shape
    lanes = adapters * rank
    half_out = out_ref.shape[1]
    tile = half_out // 2
    chunks = tile // 128
    requests = len_ref.shape[1]
    length = n // 2

    s = lax.axis_index("store")
    t = lax.axis_index("tensor")
    p = s // 2
    y = lax.rem(s, 2)
    sibling = {"tensor": 1 - t}
    partner = {"store": 2 * p + 1 - y}
    diagonal = {"store": 2 * p + 1 - y, "tensor": 1 - t}
    right = {"store": s + 2}
    left = {"store": s - 2}
    has_left = p > 0
    has_right = p < length - 1

    def columns(which, width):
        return pl.ds(pl.multiple_of(which * width, 128), width)

    local_down = pltpu.make_async_copy(down_ref, dv, loc.at[0])
    local_up = pltpu.make_async_copy(up_ref, uv, loc.at[1])
    local_x2 = pltpu.make_async_copy(
        x_ref.at[:, columns(y, quarter)], x2.at[pl.ds(0, tokens)], loc.at[2]
    )
    local_x = pltpu.make_async_copy(x_ref, xv, loc.at[3])
    local_down.start()
    local_up.start()

    def weight_copy(j):
        which = lax.rem((1 - t) * 2 + j, 4)
        return pltpu.make_async_copy(
            w_ref.at[:, columns(which, tile)], wb.at[j % 2], wsem.at[j]
        )

    barrier = pltpu.get_barrier_semaphore()
    for who in (sibling, partner, diagonal):
        pl.semaphore_signal(barrier, inc=1, device_id=who, device_id_type=MESH)

    @pl.when(has_left)
    def _():
        pl.semaphore_signal(barrier, inc=1, device_id=left, device_id_type=MESH)

    @pl.when(has_right)
    def _():
        pl.semaphore_signal(barrier, inc=1, device_id=right, device_id_type=MESH)

    def pack(which, dst):
        rows = pl.ds(pl.multiple_of(which * quarter, 128), quarter)
        for a in range(adapters):
            dst[0:quarter, a * rank:(a + 1) * rank] = dv[a, rows, :]
        width = columns(t * 2 + which, tile)
        for a in range(adapters):
            block = uv[a, :, width]
            for c in range(chunks):
                at = quarter + c * lanes + a * rank
                dst[at:at + rank, :] = block[:, c * 128:(c + 1) * 128]

    meta[...] = jnp.zeros_like(meta)
    meta[0:1, 0:requests] = len_ref[...]
    meta[1:2, 0:requests] = ids_ref[...]
    local_down.wait()
    local_up.wait()
    pack(1 - y, stage)

    def remote(src, dst, send, recv, who):
        return pltpu.make_async_remote_copy(
            src_ref=src, dst_ref=dst, send_sem=send, recv_sem=recv,
            device_id=who, device_id_type=MESH,
        )

    pair_block = remote(stage, big.at[2 * p + 1], pair_s.at[0], pair_r.at[0], partner)
    pair_meta = remote(meta, metap, pair_s.at[1], pair_r.at[1], partner)
    pair_x = remote(
        x_ref.at[:, columns(1 - y, quarter)], x2.at[pl.ds(tokens, tokens)],
        pair_s.at[2], pair_r.at[2], partner,
    )
    base_copy = remote(bsend, brecv, pair_s.at[3], pair_r.at[3], sibling)

    def line(direction, k, o):
        q = p - k if direction == 0 else p + k
        who = right if direction == 0 else left
        return remote(
            big.at[2 * q + o], big.at[2 * q + o],
            ls.at[direction, k, o], lr.at[direction, k, o], who,
        )

    def line_arrival(direction, k, o):
        q = p - k if direction == 0 else p + k
        return remote(
            big.at[2 * q + o], big.at[2 * q + o],
            ls.at[direction, k - 1, o], lr.at[direction, k - 1, o], partner,
        )

    def forward_up(q, o):
        slot = 2 * q + o
        return remote(
            big.at[slot, pl.ds(quarter, chunks * lanes)], upx.at[slot],
            us.at[slot], ur.at[slot], partner,
        )

    count = 3 + has_left.astype(jnp.int32) + has_right.astype(jnp.int32)
    pl.semaphore_wait(barrier, count)
    pair_block.start()
    pair_meta.start()
    pack(y, big.at[2 * p])

    def send_line(k, o, direction):
        @pl.when(has_right if direction == 0 else has_left)
        def _():
            line(direction, k, o).start()

    for direction in (0, 1):
        send_line(0, 0, direction)
    forward_up(p, 0).start()
    local_x.start()
    local_x2.start()
    weight_copy(0).start()
    weight_copy(1).start()

    lane_adapter = (lax.broadcasted_iota(jnp.int32, (1, lanes), 1) // rank).astype(F32)

    def project(q, o, first, rows):
        parity = y if o == 0 else 1 - y
        store = 2 * q + parity
        product = jnp.dot(
            x2[first:first + rows, :], big[2 * q + o, 0:quarter, :],
            preferred_element_type=F32,
        )
        wanted = lane_adapter + (store * adapters).astype(F32)
        keep = tok[first:first + rows, :] == wanted
        acc[first:first + rows, :] += jnp.where(keep, product, 0.0)

    def token_rows(ref, first):
        lengths_row = ref[0:1, 0:requests].astype(F32)
        ids_row = ref[1:2, 0:requests].astype(F32)
        tok[first:first + tokens, :] = jnp.broadcast_to(
            adapter_of_token(lengths_row, ids_row, tokens), (tokens, lanes)
        )

    acc[...] = jnp.zeros_like(acc)
    token_rows(meta, 0)
    local_x2.wait()
    project(p, 0, 0, tokens)
    pair_block.wait_recv()
    for direction in (0, 1):
        send_line(0, 1, direction)
    forward_up(p, 1).start()
    pair_block.wait_send()
    pair_x.start()
    project(p, 1, 0, tokens)

    local_x.wait()
    for j in range(4):
        weight_copy(j).wait()
        product = jnp.dot(xv[...], wb[j % 2], preferred_element_type=F32)
        at = (j % 2) * tile
        if j < 2:
            bsend[:, at:at + tile] = product.astype(BF16)
            weight_copy(j + 2).start()
        else:
            basev[:, at:at + tile] = product
        if j == 1:
            base_copy.start()

    def step(k, first, rows):
        for o in (0, 1):
            for direction in (0, 1):
                q = p - k if direction == 0 else p + k
                there = q >= 0 if direction == 0 else q < length

                @pl.when(there)
                def _():
                    line_arrival(direction, k, o).wait_recv()
                    send_line(k, o, direction)
                    forward_up(q, o).start()
                    project(q, o, first, rows)

    switch = min(2, length)

    def early(k, carry):
        step(k, 0, tokens)
        return carry

    lax.fori_loop(1, switch, early, 0)

    pair_meta.wait_recv()
    token_rows(metap, tokens)
    base_copy.wait_recv()
    basev[...] += brecv[...].astype(F32)
    pair_x.wait_recv()
    for o in (0, 1):
        project(p, o, tokens, tokens)
        for k in range(1, switch):
            for direction in (0, 1):
                q = p - k if direction == 0 else p + k
                there = q >= 0 if direction == 0 else q < length

                @pl.when(there)
                def _():
                    project(q, o, tokens, tokens)

    def late(k, carry):
        step(k, 0, 2 * tokens)
        return carry

    lax.fori_loop(switch, length, late, 0)

    snd[0] = acc[0:tokens, :].astype(BF16)
    snd[1] = acc[tokens:, :].astype(BF16)
    sums = [
        remote(snd.at[1], rcv.at[1], ss.at[1], sr.at[1], partner),
        remote(snd.at[1], rcv.at[2], ss.at[2], sr.at[2], diagonal),
        remote(snd.at[0], rcv.at[0], ss.at[0], sr.at[0], sibling),
    ]
    for copy in sums:
        copy.start()

    def wait_up(slot, carry):
        forward_up(slot // 2, lax.rem(slot, 2)).wait()
        return carry

    lax.fori_loop(0, n, wait_up, 0)
    for copy in sums:
        copy.wait_recv()
    shrink = acc[0:tokens, :]
    for i in range(3):
        shrink = shrink + rcv[i].astype(F32)

    def expand(q, carry):
        parts = []
        for o in (0, 1):
            parity = y if o == 0 else 1 - y
            wanted = lane_adapter + ((2 * q + parity) * adapters).astype(F32)
            parts.append(jnp.where(tok[0:tokens, :] == wanted, shrink, 0.0))
        left_hand = jnp.concatenate(parts, axis=1).astype(BF16)

        def columns_of(get, order):
            return jnp.concatenate(
                [
                    jnp.concatenate([get(2 * q + o, c) for o in order], axis=0)
                    for c in range(chunks)
                ],
                axis=1,
            )

        mine = columns_of(
            lambda slot, c: big[slot, quarter + c * lanes:quarter + (c + 1) * lanes, :], (0, 1)
        )
        theirs = columns_of(
            lambda slot, c: upx[slot, c * lanes:(c + 1) * lanes, :], (1, 0)
        )
        a, b = carry
        a = a + jnp.dot(left_hand, mine, preferred_element_type=F32)
        b = b + jnp.dot(left_hand, theirs, preferred_element_type=F32)
        return a, b

    zero = jnp.zeros((tokens, tile), F32)
    a, b = lax.fori_loop(0, length, expand, (zero, zero))
    for which, value in ((y, a), (1 - y, b)):
        at = columns(which, tile)
        total = basev[:, at] + ADAPTER_SCALE * value.astype(BF16).astype(F32)
        out_ref[:, at] = total.astype(BF16)

    def drain(k, carry):
        for o in (0, 1):
            @pl.when(has_right & (p - k >= 0))
            def _():
                line(0, k, o).wait_send()

            @pl.when(has_left & (p + k < length))
            def _():
                line(1, k, o).wait_send()

        return carry

    lax.fori_loop(0, length - 1, drain, 0)
    pair_meta.wait_send()
    pair_x.wait_send()
    base_copy.wait_send()
    for copy in sums:
        copy.wait_send()


def local(hidden_in, base_weight, adapter_down, adapter_up, lengths, adapter_ids):
    n = lax.axis_size("store")
    tokens, depth = hidden_in.shape
    quarter = depth // 2
    adapters, _, rank = adapter_down.shape
    lanes = adapters * rank
    width = adapter_up.shape[2]
    half = width // 2
    tile = half // 2
    up_rows = tile // 128 * lanes
    length = n // 2
    requests = lengths.shape[0]
    dma = pltpu.SemaphoreType.DMA
    vmem = pl.BlockSpec(memory_space=pltpu.VMEM)
    hbm = pl.BlockSpec(memory_space=pl.ANY)
    return pl.pallas_call(
        functools.partial(kernel, n),
        out_shape=jax.ShapeDtypeStruct((tokens, half), BF16),
        in_specs=[hbm, hbm, hbm, hbm, vmem, vmem],
        out_specs=vmem,
        scratch_shapes=[
            pltpu.VMEM((tokens, depth), BF16),
            pltpu.VMEM((2 * tokens, quarter), BF16),
            pltpu.VMEM((2, depth, tile), BF16),
            pltpu.VMEM((adapters, depth, rank), BF16),
            pltpu.VMEM((adapters, rank, width), BF16),
            pltpu.VMEM((quarter + up_rows, lanes), BF16),
            pltpu.VMEM((n, quarter + up_rows, lanes), BF16),
            pltpu.VMEM((n, up_rows, lanes), BF16),
            pltpu.VMEM((8, 128), jnp.int32),
            pltpu.VMEM((8, 128), jnp.int32),
            pltpu.VMEM((2 * tokens, lanes), F32),
            pltpu.VMEM((2 * tokens, lanes), F32),
            pltpu.VMEM((2, tokens, lanes), BF16),
            pltpu.VMEM((3, tokens, lanes), BF16),
            pltpu.VMEM((tokens, half), F32),
            pltpu.VMEM((tokens, half), BF16),
            pltpu.VMEM((tokens, half), BF16),
            dma((4,)),
            dma((4,)),
            dma((2, length, 2)),
            dma((2, length, 2)),
            dma((4,)),
            dma((4,)),
            dma((n,)),
            dma((n,)),
            dma((3,)),
            dma((3,)),
        ],
        compiler_params=pltpu.CompilerParams(
            collective_id=0, has_side_effects=True, vmem_limit_bytes=62 * 1024 * 1024
        ),
    )(
        hidden_in, base_weight, adapter_down, adapter_up,
        lengths.reshape(1, requests), adapter_ids.reshape(1, requests),
    )


def solution(mesh):
    return jax.shard_map(
        local,
        mesh=mesh,
        in_specs=(
            P(("groups", "store"), "tensor"),
            P("tensor", None),
            P(("groups", "store"), "tensor", None),
            P(("groups", "store"), None, None),
            P(("groups", "store")),
            P(("groups", "store")),
        ),
        out_specs=P(("groups", "store"), "tensor"),
        check_vma=False,
    )
```

```python
import functools

import jax
import jax.numpy as jnp
from jax import lax
from jax.experimental import pallas as pl
from jax.experimental.pallas import tpu as pltpu
from jax.sharding import PartitionSpec as P

ADAPTER_SCALE = 0.5
MESH = pl.DeviceIdType.MESH
F32 = jnp.float32
BF16 = jnp.bfloat16


def adapter_of_token(lengths_row, ids_row, tokens):
    count = lengths_row.shape[1]
    down = lax.broadcasted_iota(jnp.int32, (count, count), 0)
    across = lax.broadcasted_iota(jnp.int32, (count, count), 1)
    column = jnp.sum(jnp.where(down == across, lengths_row, 0.0), axis=1, keepdims=True)
    ends = jnp.sum(jnp.where(down <= across, column, 0.0), axis=0, keepdims=True)
    starts = ends - lengths_row
    token = lax.broadcasted_iota(jnp.int32, (tokens, count), 0).astype(F32)
    inside = (token >= starts) & (token < ends)
    return jnp.sum(jnp.where(inside, ids_row, 0.0), axis=1, keepdims=True)


def pack(value, rank):
    folded = value + pltpu.roll(value, rank, 1)
    rows = value.shape[0] // 2
    low = lax.broadcasted_iota(jnp.int32, (rows, 2 * rank), 1) < rank
    return jnp.where(low, folded[:rows], folded[rows:]).astype(BF16)


def unpack(value, rank):
    value = value.astype(F32)
    turned = pltpu.roll(value, rank, 1)
    low = lax.broadcasted_iota(jnp.int32, value.shape, 1) < rank
    return jnp.concatenate(
        [jnp.where(low, value, turned), jnp.where(low, turned, value)], axis=0
    )


def kernel(
    n, rank, x_ref, w_ref, down_ref, up_ref, len_ref, ids_ref, out_ref,
    xv, x2c, x2e, xe, wb, big, bigb, upx, meta, metap, metae, tok, toke, acc, acce,
    snd, rcv, snde, rcve, basev, bsend, brecv,
    loc, wsem, ls, lr, bs, br, pair_s, pair_r, us, ur, ss, sr, es, er,
):
    tokens = x_ref.shape[0]
    quarter = x_ref.shape[1] // 2
    lanes = down_ref.shape[0]
    adapters = lanes // rank
    extra = x2e.shape[1]
    common = x2c.shape[1]
    half_out = out_ref.shape[1]
    tile = half_out // 2
    requests = len_ref.shape[1]
    length = n // 2

    s = lax.axis_index("store")
    t = lax.axis_index("tensor")
    p = s // 2
    y = lax.rem(s, 2)
    sibling = {"tensor": 1 - t}
    partner = {"store": 2 * p + 1 - y}
    diagonal = {"store": 2 * p + 1 - y, "tensor": 1 - t}
    right = {"store": s + 2}
    left = {"store": s - 2}
    has_left = p > 0
    has_right = p < length - 1
    is_end = (p == 0) | (p == length - 1)
    is_inner = (p > 0) & (p < length - 1)
    is_helper = (p == 1) | (p == length - 2)
    peer = {"store": s + jnp.where((p == 0) | (p == length - 2), 2, -2)}

    def columns(which, width):
        return pl.ds(pl.multiple_of(which * width, 128), width)

    def common_of(which):
        return pl.ds(pl.multiple_of(which * quarter, 128), common)

    def extra_of(which):
        return pl.ds(pl.multiple_of(which * quarter + common, 128), extra)

    own_rows = pl.ds(0, tokens)
    other_rows = pl.ds(tokens, tokens)
    down_part = (slice(None), pl.ds(0, common))
    up_part = (slice(None), pl.ds(common, tile))

    def local_copy(src, dst, i):
        return pltpu.make_async_copy(src, dst, loc.at[i])

    local_a = local_copy(down_ref.at[:, common_of(y)], big.at[(2 * p,) + down_part], 0)
    local_u = local_copy(up_ref.at[:, columns(t * 2 + y, tile)], big.at[(2 * p,) + up_part], 1)
    local_b = local_copy(down_ref.at[:, extra_of(y)], bigb.at[2 * p], 2)
    local_xe = local_copy(x_ref.at[:, extra_of(y)], x2e.at[own_rows], 3)
    local_xc = local_copy(x_ref.at[:, common_of(y)], x2c.at[own_rows], 4)
    local_x = local_copy(x_ref, xv, 5)

    def weight_copy(j):
        which = lax.rem((1 - t) * 2 + j, 4)
        return pltpu.make_async_copy(
            w_ref.at[:, columns(which, tile)], wb.at[j % 2], wsem.at[j]
        )

    barrier = pltpu.get_barrier_semaphore()
    for who in (sibling, partner, diagonal):
        pl.semaphore_signal(barrier, inc=1, device_id=who, device_id_type=MESH)

    @pl.when(has_left)
    def _():
        pl.semaphore_signal(barrier, inc=1, device_id=left, device_id_type=MESH)

    @pl.when(has_right)
    def _():
        pl.semaphore_signal(barrier, inc=1, device_id=right, device_id_type=MESH)

    for copy in (local_a, local_u, local_b, local_xe, local_xc, local_x):
        copy.start()
    weight_copy(0).start()
    weight_copy(1).start()
    meta[...] = jnp.zeros_like(meta)
    meta[0:1, 0:requests] = len_ref[...]
    meta[1:2, 0:requests] = ids_ref[...]

    def remote(src, dst, send, recv, who):
        return pltpu.make_async_remote_copy(
            src_ref=src, dst_ref=dst, send_sem=send, recv_sem=recv,
            device_id=who, device_id_type=MESH,
        )

    def pair_copy(src, dst, i, who=partner):
        return remote(src, dst, pair_s.at[i], pair_r.at[i], who)

    pair_a = pair_copy(down_ref.at[:, common_of(1 - y)], big.at[(2 * p + 1,) + down_part], 0)
    pair_u = pair_copy(
        up_ref.at[:, columns(t * 2 + 1 - y, tile)], big.at[(2 * p + 1,) + up_part], 1
    )
    pair_meta = pair_copy(meta, metap, 2)
    pair_xe = pair_copy(x_ref.at[:, extra_of(1 - y)], x2e.at[other_rows], 3)
    pair_b = pair_copy(down_ref.at[:, extra_of(1 - y)], bigb.at[2 * p + 1], 4)
    pair_xc = pair_copy(x_ref.at[:, common_of(1 - y)], x2c.at[other_rows], 5)
    base_copy = pair_copy(bsend, brecv, 6, sibling)

    def end_copy(src, dst, i):
        return remote(src, dst, es.at[i], er.at[i], peer)

    end_x = [
        end_copy(x2e.at[own_rows], xe.at[own_rows], 0),
        end_copy(x2e.at[other_rows], xe.at[other_rows], 1),
    ]
    end_meta = [end_copy(meta, metae.at[0], 2), end_copy(metap, metae.at[1], 3)]
    end_sum = end_copy(snde, rcve, 4)

    def position(direction, k):
        return p - k if direction == 0 else p + k

    def inside(direction, k):
        return position(direction, k) >= 0 if direction == 0 else position(direction, k) < length

    def line(buffer, send, recv, direction, k, o):
        slot = buffer.at[2 * position(direction, k) + o]
        return remote(
            slot, slot, send.at[direction, k, o], recv.at[direction, k, o],
            right if direction == 0 else left,
        )

    def arrival(buffer, send, recv, direction, k, o):
        slot = buffer.at[2 * position(direction, k) + o]
        return remote(
            slot, slot, send.at[direction, k - 1, o], recv.at[direction, k - 1, o], partner
        )

    goes = (has_right, has_left)
    goes_b = (p < length - 2, p > 1)

    def send_a(k, o, direction):
        @pl.when(goes[direction])
        def _():
            line(big, ls, lr, direction, k, o).start()

    def send_b(k, o, direction):
        @pl.when(goes_b[direction])
        def _():
            line(bigb, bs, br, direction, k, o).start()

    def forward_up(slot):
        return remote(big.at[(slot,) + up_part], upx.at[slot], us.at[slot], ur.at[slot], partner)

    lane_adapter = (lax.broadcasted_iota(jnp.int32, (1, lanes), 1) // rank).astype(F32)

    def wanted(q, o):
        store = 2 * q + (y if o == 0 else 1 - y)
        return lane_adapter + (store * adapters).astype(F32)

    def product(q, x, buffer, width, adapter):
        weights = buffer[pl.ds(2 * q, 2), :, 0:width].reshape(2 * lanes, width)
        full = lax.dot_general(
            x, weights, (((1,), (1,)), ((), ())), preferred_element_type=F32
        )
        return jnp.where(adapter == wanted(q, 0), full[:, 0:lanes], 0.0) + jnp.where(
            adapter == wanted(q, 1), full[:, lanes:], 0.0
        )

    def project_a(q, first):
        rows = slice(first, first + tokens)
        acc[rows, :] += product(q, x2c[rows, :], big, common, tok[rows, :])

    def project_b(q, first):
        rows = slice(first, first + tokens)
        acc[rows, :] += product(q, x2e[rows, :], bigb, extra, tok[rows, :])

    def token_rows(ref, dst, first):
        lengths_row = ref[0:1, 0:requests].astype(F32)
        ids_row = ref[1:2, 0:requests].astype(F32)
        dst[first:first + tokens, :] = jnp.broadcast_to(
            adapter_of_token(lengths_row, ids_row, tokens), (tokens, lanes)
        )

    count = 3 + has_left.astype(jnp.int32) + has_right.astype(jnp.int32)
    pl.semaphore_wait(barrier, count)
    pair_a.start()
    pair_u.start()
    pair_meta.start()
    local_a.wait()
    local_u.wait()
    for direction in (0, 1):
        send_a(0, 0, direction)
    forward_up(2 * p).start()
    acc[...] = jnp.zeros_like(acc)
    token_rows(meta, tok, 0)
    local_b.wait()
    local_xe.wait()
    local_xc.wait()
    pair_a.wait_recv()
    pair_u.wait_recv()
    for direction in (0, 1):
        send_a(0, 1, direction)
    forward_up(2 * p + 1).start()
    pair_a.wait_send()
    pair_u.wait_send()
    pair_xe.start()

    @pl.when(is_end)
    def _():
        end_meta[0].start()
        end_x[0].start()

    project_a(p, 0)

    local_x.wait()
    for j in range(4):
        weight_copy(j).wait()
        part = jnp.dot(xv[...], wb[j % 2], preferred_element_type=F32)
        at = (j % 2) * tile
        if j < 2:
            bsend[:, at:at + tile] = part.astype(BF16)
            weight_copy(j + 2).start()
        else:
            basev[:, at:at + tile] = part
        if j == 1:
            base_copy.start()

    def step_a(k):
        for o in (0, 1):
            for direction in (0, 1):
                @pl.when(inside(direction, k))
                def _():
                    arrival(big, ls, lr, direction, k, o).wait_recv()
                    send_a(k, o, direction)
                    forward_up(2 * position(direction, k) + o).start()

        for direction in (0, 1):
            @pl.when(inside(direction, k))
            def _():
                project_a(position(direction, k), 0)

    step_a(1)
    pair_xe.wait_send()
    pair_b.start()
    pair_xc.start()
    pair_meta.wait_recv()
    token_rows(metap, tok, tokens)
    base_copy.wait_recv()
    basev[...] += brecv[...].astype(F32)
    pair_xe.wait_recv()

    @pl.when(is_end)
    def _():
        for direction in (0, 1):
            send_b(0, 0, direction)
        end_meta[1].start()
        end_x[1].start()

    pair_b.wait_recv()

    @pl.when(is_end)
    def _():
        for direction in (0, 1):
            send_b(0, 1, direction)

    def loop_a(k, carry):
        step_a(k)
        return carry

    lax.fori_loop(2, length, loop_a, 0)

    @pl.when(is_inner)
    def _():
        for o in (0, 1):
            for direction in (0, 1):
                send_b(0, o, direction)
        project_b(p, 0)

        def loop_b(k, carry):
            for o in (0, 1):
                for direction in (0, 1):
                    @pl.when(inside(direction, k))
                    def _():
                        arrival(bigb, bs, br, direction, k, o).wait_recv()
                        send_b(k, o, direction)

            for direction in (0, 1):
                @pl.when(inside(direction, k))
                def _():
                    project_b(position(direction, k), 0)

            return carry

        lax.fori_loop(1, length - 1, loop_b, 0)

    @pl.when(is_helper)
    def _():
        for copy in end_meta + end_x:
            copy.wait_recv()
        for i in (0, 1):
            token_rows(metae.at[i], toke, i * tokens)
        acce[...] = jnp.zeros_like(acce)

        def loop_e(q, carry):
            acce[...] += product(q, xe[...], bigb, extra, toke[...])
            return carry

        lax.fori_loop(0, length, loop_e, 0)
        for i in (0, 1):
            snde[i] = pack(acce[i * tokens:(i + 1) * tokens, :], rank)
        end_sum.start()

    pair_xc.wait_recv()

    def loop_partner(q, carry):
        project_a(q, tokens)

        @pl.when(is_inner)
        def _():
            project_b(q, tokens)

        return carry

    lax.fori_loop(0, length, loop_partner, 0)

    @pl.when(is_end)
    def _():
        end_sum.wait_recv()
        for i in (0, 1):
            rows = slice(i * tokens, (i + 1) * tokens)
            parity = tok[rows, :] - 2.0 * jnp.floor(tok[rows, :] * 0.5)
            acc[rows, :] += jnp.where(parity == lane_adapter, unpack(rcve[i], rank), 0.0)

    snd[1] = pack(acc[tokens:, :], rank)
    snd[0] = pack(acc[0:tokens, :], rank)
    sums = [
        remote(snd.at[1], rcv.at[2], ss.at[2], sr.at[2], diagonal),
        remote(snd.at[1], rcv.at[1], ss.at[1], sr.at[1], partner),
        remote(snd.at[0], rcv.at[0], ss.at[0], sr.at[0], sibling),
    ]
    for copy in sums:
        copy.start()

    def wait_up(slot, carry):
        forward_up(slot).wait()
        return carry

    lax.fori_loop(0, n, wait_up, 0)
    for copy in sums:
        copy.wait_recv()
    shrink = acc[0:tokens, :]
    for i in range(3):
        shrink = shrink + unpack(rcv[i], rank)
    own_adapter = tok[0:tokens, :]

    def expand(q, carry):
        parts = [jnp.where(own_adapter == wanted(q, o), shrink, 0.0) for o in (0, 1)]
        rows = jnp.concatenate(parts, axis=1).astype(BF16)
        mine = big[pl.ds(2 * q, 2), :, common:common + tile].reshape(2 * lanes, tile)
        theirs = jnp.concatenate([upx[2 * q + 1], upx[2 * q]], axis=0)
        a, b = carry
        a = a + jnp.dot(rows, mine, preferred_element_type=F32)
        b = b + jnp.dot(rows, theirs, preferred_element_type=F32)
        return a, b

    zero = jnp.zeros((tokens, tile), F32)
    a, b = lax.fori_loop(0, length, expand, (zero, zero))
    for which, value in ((y, a), (1 - y, b)):
        at = columns(which, tile)
        total = basev[:, at] + ADAPTER_SCALE * value.astype(BF16).astype(F32)
        out_ref[:, at] = total.astype(BF16)

    def drain(k, carry):
        for o in (0, 1):
            for direction in (0, 1):
                @pl.when(goes[direction] & inside(direction, k))
                def _():
                    line(big, ls, lr, direction, k, o).wait_send()

                @pl.when(goes_b[direction] & inside(direction, k))
                def _():
                    line(bigb, bs, br, direction, k, o).wait_send()

        return carry

    lax.fori_loop(0, length - 1, drain, 0)

    @pl.when(is_end)
    def _():
        for copy in end_meta + end_x:
            copy.wait_send()

    @pl.when(is_helper)
    def _():
        end_sum.wait_send()

    for copy in [pair_meta, pair_b, pair_xc, base_copy] + sums:
        copy.wait_send()


def local(hidden_in, base_weight, adapter_down, adapter_up, lengths, adapter_ids):
    n = lax.axis_size("store")
    tokens, depth = hidden_in.shape
    quarter = depth // 2
    adapters, _, rank = adapter_down.shape
    lanes = adapters * rank
    width = adapter_up.shape[2]
    half = width // 2
    tile = half // 2
    length = n // 2
    assert length >= 4 and adapters == 2
    extra = quarter * 3 // 8 // 128 * 128
    common = quarter - extra
    requests = lengths.shape[0]
    dma = pltpu.SemaphoreType.DMA
    vmem = pl.BlockSpec(memory_space=pltpu.VMEM)
    hbm = pl.BlockSpec(memory_space=pl.ANY)
    return pl.pallas_call(
        functools.partial(kernel, n, rank),
        out_shape=jax.ShapeDtypeStruct((tokens, half), BF16),
        in_specs=[hbm, hbm, hbm, hbm, vmem, vmem],
        out_specs=vmem,
        scratch_shapes=[
            pltpu.VMEM((tokens, depth), BF16),
            pltpu.VMEM((2 * tokens, common), BF16),
            pltpu.VMEM((2 * tokens, extra), BF16),
            pltpu.VMEM((2 * tokens, extra), BF16),
            pltpu.VMEM((2, depth, tile), BF16),
            pltpu.VMEM((n, lanes, common + tile), BF16),
            pltpu.VMEM((n, lanes, extra), BF16),
            pltpu.VMEM((n, lanes, tile), BF16),
            pltpu.VMEM((8, 128), jnp.int32),
            pltpu.VMEM((8, 128), jnp.int32),
            pltpu.VMEM((2, 8, 128), jnp.int32),
            pltpu.VMEM((2 * tokens, lanes), F32),
            pltpu.VMEM((2 * tokens, lanes), F32),
            pltpu.VMEM((2 * tokens, lanes), F32),
            pltpu.VMEM((2 * tokens, lanes), F32),
            pltpu.VMEM((2, tokens // 2, lanes), BF16),
            pltpu.VMEM((3, tokens // 2, lanes), BF16),
            pltpu.VMEM((2, tokens // 2, lanes), BF16),
            pltpu.VMEM((2, tokens // 2, lanes), BF16),
            pltpu.VMEM((tokens, half), F32),
            pltpu.VMEM((tokens, half), BF16),
            pltpu.VMEM((tokens, half), BF16),
            dma((6,)),
            dma((4,)),
            dma((2, length, 2)),
            dma((2, length, 2)),
            dma((2, length, 2)),
            dma((2, length, 2)),
            dma((7,)),
            dma((7,)),
            dma((n,)),
            dma((n,)),
            dma((3,)),
            dma((3,)),
            dma((5,)),
            dma((5,)),
        ],
        compiler_params=pltpu.CompilerParams(
            collective_id=0, has_side_effects=True, vmem_limit_bytes=62 * 1024 * 1024
        ),
    )(
        hidden_in, base_weight,
        adapter_down.transpose(0, 2, 1).reshape(lanes, depth),
        adapter_up.reshape(lanes, width),
        lengths.reshape(1, requests), adapter_ids.reshape(1, requests),
    )


def solution(mesh):
    return jax.shard_map(
        local,
        mesh=mesh,
        in_specs=(
            P(("groups", "store"), "tensor"),
            P("tensor", None),
            P(("groups", "store"), "tensor", None),
            P(("groups", "store"), None, None),
            P(("groups", "store")),
            P(("groups", "store")),
        ),
        out_specs=P(("groups", "store"), "tensor"),
        check_vma=False,
    )
```

```python
import functools

import jax
import jax.numpy as jnp
from jax import lax
from jax.experimental import pallas as pl
from jax.experimental.pallas import tpu as pltpu
from jax.sharding import PartitionSpec as P

ADAPTER_SCALE = 0.5
MESH = pl.DeviceIdType.MESH
F32 = jnp.float32
BF16 = jnp.bfloat16


def adapter_of_token(lengths_row, ids_row, tokens):
    count = lengths_row.shape[1]
    down = lax.broadcasted_iota(jnp.int32, (count, count), 0)
    across = lax.broadcasted_iota(jnp.int32, (count, count), 1)
    column = jnp.sum(jnp.where(down == across, lengths_row, 0.0), axis=1, keepdims=True)
    ends = jnp.sum(jnp.where(down <= across, column, 0.0), axis=0, keepdims=True)
    starts = ends - lengths_row
    token = lax.broadcasted_iota(jnp.int32, (tokens, count), 0).astype(F32)
    inside = (token >= starts) & (token < ends)
    return jnp.sum(jnp.where(inside, ids_row, 0.0), axis=1, keepdims=True)


def pack(value, rank):
    folded = value + pltpu.roll(value, rank, 1)
    rows = value.shape[0] // 2
    low = lax.broadcasted_iota(jnp.int32, (rows, 2 * rank), 1) < rank
    return jnp.where(low, folded[:rows], folded[rows:]).astype(BF16)


def unpack(value, rank):
    value = value.astype(F32)
    turned = pltpu.roll(value, rank, 1)
    low = lax.broadcasted_iota(jnp.int32, value.shape, 1) < rank
    return jnp.concatenate(
        [jnp.where(low, value, turned), jnp.where(low, turned, value)], axis=0
    )


def kernel(
    n, rank, x_ref, w_ref, down_ref, up_ref, len_ref, ids_ref, out_ref,
    xv, x2c, x2e, xe, wb, big, bigb, upx, meta, metap, metae, tok, toke, acc, acce,
    snd, rcv, snde, rcve, basev, bsend, brecv,
    loc, wsem, ls, lr, bs, br, pair_s, pair_r, us, ur, ss, sr, es, er,
):
    tokens = x_ref.shape[0]
    quarter = x_ref.shape[1] // 2
    lanes = down_ref.shape[0]
    adapters = lanes // rank
    extra = x2e.shape[1]
    common = x2c.shape[1]
    half_out = out_ref.shape[1]
    tile = half_out // 2
    requests = len_ref.shape[1]
    length = n // 2

    s = lax.axis_index("store")
    t = lax.axis_index("tensor")
    p = s // 2
    y = lax.rem(s, 2)
    sibling = {"tensor": 1 - t}
    partner = {"store": 2 * p + 1 - y}
    diagonal = {"store": 2 * p + 1 - y, "tensor": 1 - t}
    right = {"store": s + 2}
    left = {"store": s - 2}
    has_left = p > 0
    has_right = p < length - 1
    is_end = (p == 0) | (p == length - 1)
    is_inner = (p > 0) & (p < length - 1)
    is_helper = (p == 1) | (p == length - 2)
    peer = {"store": s + jnp.where((p == 0) | (p == length - 2), 2, -2)}

    def columns(which, width):
        return pl.ds(pl.multiple_of(which * width, 128), width)

    def common_of(which):
        return pl.ds(pl.multiple_of(which * quarter, 128), common)

    def extra_of(which):
        return pl.ds(pl.multiple_of(which * quarter + common, 128), extra)

    own_rows = pl.ds(0, tokens)
    other_rows = pl.ds(tokens, tokens)
    down_part = (slice(None), pl.ds(0, common))
    up_part = (slice(None), pl.ds(common, tile))

    def local_copy(src, dst, i):
        return pltpu.make_async_copy(src, dst, loc.at[i])

    local_a = local_copy(down_ref.at[:, common_of(y)], big.at[(2 * p,) + down_part], 0)
    local_u = local_copy(up_ref.at[:, columns(t * 2 + y, tile)], big.at[(2 * p,) + up_part], 1)
    local_b = local_copy(down_ref.at[:, extra_of(y)], bigb.at[2 * p], 2)
    local_xe = local_copy(x_ref.at[:, extra_of(y)], x2e.at[own_rows], 3)
    local_xc = local_copy(x_ref.at[:, common_of(y)], x2c.at[own_rows], 4)
    local_x = local_copy(x_ref, xv, 5)

    def weight_copy(j):
        which = lax.rem((1 - t) * 2 + j, 4)
        return pltpu.make_async_copy(
            w_ref.at[:, columns(which, tile)], wb.at[j % 2], wsem.at[j]
        )

    barrier = pltpu.get_barrier_semaphore()
    for who in (sibling, partner, diagonal):
        pl.semaphore_signal(barrier, inc=1, device_id=who, device_id_type=MESH)

    @pl.when(has_left)
    def _():
        pl.semaphore_signal(barrier, inc=1, device_id=left, device_id_type=MESH)

    @pl.when(has_right)
    def _():
        pl.semaphore_signal(barrier, inc=1, device_id=right, device_id_type=MESH)

    for copy in (local_a, local_u, local_b, local_xe, local_xc, local_x):
        copy.start()
    weight_copy(0).start()
    weight_copy(1).start()
    meta[...] = jnp.zeros_like(meta)
    meta[0:1, 0:requests] = len_ref[...]
    meta[1:2, 0:requests] = ids_ref[...]

    def remote(src, dst, send, recv, who):
        return pltpu.make_async_remote_copy(
            src_ref=src, dst_ref=dst, send_sem=send, recv_sem=recv,
            device_id=who, device_id_type=MESH,
        )

    def pair_copy(src, dst, i, who=partner):
        return remote(src, dst, pair_s.at[i], pair_r.at[i], who)

    pair_a = pair_copy(down_ref.at[:, common_of(1 - y)], big.at[(2 * p + 1,) + down_part], 0)
    pair_u = pair_copy(
        up_ref.at[:, columns(t * 2 + 1 - y, tile)], big.at[(2 * p + 1,) + up_part], 1
    )
    pair_meta = pair_copy(meta, metap, 2)
    pair_xe = pair_copy(x_ref.at[:, extra_of(1 - y)], x2e.at[other_rows], 3)
    pair_b = pair_copy(down_ref.at[:, extra_of(1 - y)], bigb.at[2 * p + 1], 4)
    pair_xc = pair_copy(x_ref.at[:, common_of(1 - y)], x2c.at[other_rows], 5)
    base_copy = pair_copy(bsend, brecv, 6, sibling)

    def end_copy(src, dst, i):
        return remote(src, dst, es.at[i], er.at[i], peer)

    end_x = [
        end_copy(x2e.at[own_rows], xe.at[own_rows], 0),
        end_copy(x2e.at[other_rows], xe.at[other_rows], 1),
    ]
    end_meta = [end_copy(meta, metae.at[0], 2), end_copy(metap, metae.at[1], 3)]
    end_sum = end_copy(snde, rcve, 4)

    def position(direction, k):
        return p - k if direction == 0 else p + k

    def inside(direction, k):
        return position(direction, k) >= 0 if direction == 0 else position(direction, k) < length

    def line(buffer, send, recv, direction, k, o):
        slot = buffer.at[2 * position(direction, k) + o]
        return remote(
            slot, slot, send.at[direction, k, o], recv.at[direction, k, o],
            right if direction == 0 else left,
        )

    def arrival(buffer, send, recv, direction, k, o):
        slot = buffer.at[2 * position(direction, k) + o]
        return remote(
            slot, slot, send.at[direction, k - 1, o], recv.at[direction, k - 1, o], partner
        )

    goes = (has_right, has_left)
    goes_b = (p < length - 2, p > 1)

    def send_a(k, o, direction):
        @pl.when(goes[direction])
        def _():
            line(big, ls, lr, direction, k, o).start()

    def send_b(k, o, direction):
        @pl.when(goes_b[direction])
        def _():
            line(bigb, bs, br, direction, k, o).start()

    def forward_up(slot):
        return remote(big.at[(slot,) + up_part], upx.at[slot], us.at[slot], ur.at[slot], partner)

    lane_adapter = (lax.broadcasted_iota(jnp.int32, (1, lanes), 1) // rank).astype(F32)

    def wanted(q, o):
        store = 2 * q + (y if o == 0 else 1 - y)
        return lane_adapter + (store * adapters).astype(F32)

    def product(q, x, buffer, width, adapter):
        weights = buffer[pl.ds(2 * q, 2), :, 0:width].reshape(2 * lanes, width)
        full = lax.dot_general(
            x, weights, (((1,), (1,)), ((), ())), preferred_element_type=F32
        )
        return jnp.where(adapter == wanted(q, 0), full[:, 0:lanes], 0.0) + jnp.where(
            adapter == wanted(q, 1), full[:, lanes:], 0.0
        )

    def project_a(q, first):
        rows = slice(first, first + tokens)
        acc[rows, :] += product(q, x2c[rows, :], big, common, tok[rows, :])

    def project_b(q, first):
        rows = slice(first, first + tokens)
        acc[rows, :] += product(q, x2e[rows, :], bigb, extra, tok[rows, :])

    def token_rows(ref, dst, first):
        lengths_row = ref[0:1, 0:requests].astype(F32)
        ids_row = ref[1:2, 0:requests].astype(F32)
        dst[first:first + tokens, :] = jnp.broadcast_to(
            adapter_of_token(lengths_row, ids_row, tokens), (tokens, lanes)
        )

    count = 3 + has_left.astype(jnp.int32) + has_right.astype(jnp.int32)
    pl.semaphore_wait(barrier, count)
    pair_a.start()
    pair_u.start()
    pair_meta.start()
    local_a.wait()
    local_u.wait()
    for direction in (0, 1):
        send_a(0, 0, direction)
    forward_up(2 * p).start()
    acc[...] = jnp.zeros_like(acc)
    token_rows(meta, tok, 0)
    local_b.wait()
    local_xe.wait()
    local_xc.wait()
    pair_a.wait_recv()
    pair_u.wait_recv()
    for direction in (0, 1):
        send_a(0, 1, direction)
    forward_up(2 * p + 1).start()
    pair_a.wait_send()
    pair_u.wait_send()
    pair_b.start()
    pair_xe.start()
    project_a(p, 0)

    local_x.wait()
    for j in range(4):
        weight_copy(j).wait()
        part = jnp.dot(xv[...], wb[j % 2], preferred_element_type=F32)
        at = (j % 2) * tile
        if j < 2:
            bsend[:, at:at + tile] = part.astype(BF16)
            weight_copy(j + 2).start()
        else:
            basev[:, at:at + tile] = part
        if j == 1:
            base_copy.start()

    def step_a(k):
        for o in (0, 1):
            for direction in (0, 1):
                @pl.when(inside(direction, k))
                def _():
                    arrival(big, ls, lr, direction, k, o).wait_recv()
                    send_a(k, o, direction)
                    forward_up(2 * position(direction, k) + o).start()

        for direction in (0, 1):
            @pl.when(inside(direction, k))
            def _():
                project_a(position(direction, k), 0)

    @pl.when(is_end)
    def _():
        end_meta[0].start()
        end_x[0].start()

    step_a(1)
    pair_b.wait_recv()

    @pl.when(is_end)
    def _():
        for o in (0, 1):
            for direction in (0, 1):
                send_b(0, o, direction)

    pair_xe.wait_send()
    pair_xc.start()
    pair_meta.wait_recv()
    token_rows(metap, tok, tokens)
    base_copy.wait_recv()
    basev[...] += brecv[...].astype(F32)
    pair_xe.wait_recv()

    @pl.when(is_end)
    def _():
        end_meta[1].start()
        end_x[1].start()

    def loop_a(k, carry):
        step_a(k)
        return carry

    lax.fori_loop(2, length, loop_a, 0)

    @pl.when(is_inner)
    def _():
        for o in (0, 1):
            for direction in (0, 1):
                send_b(0, o, direction)
        project_b(p, 0)

        def loop_b(k, carry):
            for o in (0, 1):
                for direction in (0, 1):
                    @pl.when(inside(direction, k))
                    def _():
                        arrival(bigb, bs, br, direction, k, o).wait_recv()
                        send_b(k, o, direction)

            for direction in (0, 1):
                @pl.when(inside(direction, k))
                def _():
                    project_b(position(direction, k), 0)

            return carry

        lax.fori_loop(1, length - 1, loop_b, 0)

    @pl.when(is_helper)
    def _():
        for copy in end_meta + end_x:
            copy.wait_recv()
        for i in (0, 1):
            token_rows(metae.at[i], toke, i * tokens)
        acce[...] = jnp.zeros_like(acce)

        def loop_e(q, carry):
            acce[...] += product(q, xe[...], bigb, extra, toke[...])
            return carry

        lax.fori_loop(0, length, loop_e, 0)
        for i in (0, 1):
            snde[i] = pack(acce[i * tokens:(i + 1) * tokens, :], rank)
        end_sum.start()

    pair_xc.wait_recv()

    def loop_partner(q, carry):
        project_a(q, tokens)

        @pl.when(is_inner)
        def _():
            project_b(q, tokens)

        return carry

    lax.fori_loop(0, length, loop_partner, 0)

    @pl.when(is_end)
    def _():
        end_sum.wait_recv()
        for i in (0, 1):
            rows = slice(i * tokens, (i + 1) * tokens)
            parity = tok[rows, :] - 2.0 * jnp.floor(tok[rows, :] * 0.5)
            acc[rows, :] += jnp.where(parity == lane_adapter, unpack(rcve[i], rank), 0.0)

    snd[1] = pack(acc[tokens:, :], rank)
    snd[0] = pack(acc[0:tokens, :], rank)
    sums = [
        remote(snd.at[1], rcv.at[2], ss.at[2], sr.at[2], diagonal),
        remote(snd.at[1], rcv.at[1], ss.at[1], sr.at[1], partner),
        remote(snd.at[0], rcv.at[0], ss.at[0], sr.at[0], sibling),
    ]
    for copy in sums:
        copy.start()

    def wait_up(slot, carry):
        forward_up(slot).wait()
        return carry

    lax.fori_loop(0, n, wait_up, 0)
    for copy in sums:
        copy.wait_recv()
    shrink = acc[0:tokens, :]
    for i in range(3):
        shrink = shrink + unpack(rcv[i], rank)
    own_adapter = tok[0:tokens, :]

    def expand(q, carry):
        parts = [jnp.where(own_adapter == wanted(q, o), shrink, 0.0) for o in (0, 1)]
        rows = jnp.concatenate(parts, axis=1).astype(BF16)
        mine = big[pl.ds(2 * q, 2), :, common:common + tile].reshape(2 * lanes, tile)
        theirs = jnp.concatenate([upx[2 * q + 1], upx[2 * q]], axis=0)
        a, b = carry
        a = a + jnp.dot(rows, mine, preferred_element_type=F32)
        b = b + jnp.dot(rows, theirs, preferred_element_type=F32)
        return a, b

    zero = jnp.zeros((tokens, tile), F32)
    a, b = lax.fori_loop(0, length, expand, (zero, zero))
    for which, value in ((y, a), (1 - y, b)):
        at = columns(which, tile)
        total = basev[:, at] + ADAPTER_SCALE * value.astype(BF16).astype(F32)
        out_ref[:, at] = total.astype(BF16)

    def drain(k, carry):
        for o in (0, 1):
            for direction in (0, 1):
                @pl.when(goes[direction] & inside(direction, k))
                def _():
                    line(big, ls, lr, direction, k, o).wait_send()

                @pl.when(goes_b[direction] & inside(direction, k))
                def _():
                    line(bigb, bs, br, direction, k, o).wait_send()

        return carry

    lax.fori_loop(0, length - 1, drain, 0)

    @pl.when(is_end)
    def _():
        for copy in end_meta + end_x:
            copy.wait_send()

    @pl.when(is_helper)
    def _():
        end_sum.wait_send()

    for copy in [pair_meta, pair_b, pair_xc, base_copy] + sums:
        copy.wait_send()


def local(hidden_in, base_weight, adapter_down, adapter_up, lengths, adapter_ids):
    n = lax.axis_size("store")
    tokens, depth = hidden_in.shape
    quarter = depth // 2
    adapters, _, rank = adapter_down.shape
    lanes = adapters * rank
    width = adapter_up.shape[2]
    half = width // 2
    tile = half // 2
    length = n // 2
    assert length >= 4 and adapters == 2
    extra = quarter * 5 // 16 // 128 * 128
    common = quarter - extra
    requests = lengths.shape[0]
    dma = pltpu.SemaphoreType.DMA
    vmem = pl.BlockSpec(memory_space=pltpu.VMEM)
    hbm = pl.BlockSpec(memory_space=pl.ANY)
    return pl.pallas_call(
        functools.partial(kernel, n, rank),
        out_shape=jax.ShapeDtypeStruct((tokens, half), BF16),
        in_specs=[hbm, hbm, hbm, hbm, vmem, vmem],
        out_specs=vmem,
        scratch_shapes=[
            pltpu.VMEM((tokens, depth), BF16),
            pltpu.VMEM((2 * tokens, common), BF16),
            pltpu.VMEM((2 * tokens, extra), BF16),
            pltpu.VMEM((2 * tokens, extra), BF16),
            pltpu.VMEM((2, depth, tile), BF16),
            pltpu.VMEM((n, lanes, common + tile), BF16),
            pltpu.VMEM((n, lanes, extra), BF16),
            pltpu.VMEM((n, lanes, tile), BF16),
            pltpu.VMEM((8, 128), jnp.int32),
            pltpu.VMEM((8, 128), jnp.int32),
            pltpu.VMEM((2, 8, 128), jnp.int32),
            pltpu.VMEM((2 * tokens, lanes), F32),
            pltpu.VMEM((2 * tokens, lanes), F32),
            pltpu.VMEM((2 * tokens, lanes), F32),
            pltpu.VMEM((2 * tokens, lanes), F32),
            pltpu.VMEM((2, tokens // 2, lanes), BF16),
            pltpu.VMEM((3, tokens // 2, lanes), BF16),
            pltpu.VMEM((2, tokens // 2, lanes), BF16),
            pltpu.VMEM((2, tokens // 2, lanes), BF16),
            pltpu.VMEM((tokens, half), F32),
            pltpu.VMEM((tokens, half), BF16),
            pltpu.VMEM((tokens, half), BF16),
            dma((6,)),
            dma((4,)),
            dma((2, length, 2)),
            dma((2, length, 2)),
            dma((2, length, 2)),
            dma((2, length, 2)),
            dma((7,)),
            dma((7,)),
            dma((n,)),
            dma((n,)),
            dma((3,)),
            dma((3,)),
            dma((5,)),
            dma((5,)),
        ],
        compiler_params=pltpu.CompilerParams(
            collective_id=0, has_side_effects=True, vmem_limit_bytes=62 * 1024 * 1024
        ),
    )(
        hidden_in, base_weight,
        adapter_down.transpose(0, 2, 1).reshape(lanes, depth),
        adapter_up.reshape(lanes, width),
        lengths.reshape(1, requests), adapter_ids.reshape(1, requests),
    )


def solution(mesh):
    return jax.shard_map(
        local,
        mesh=mesh,
        in_specs=(
            P(("groups", "store"), "tensor"),
            P("tensor", None),
            P(("groups", "store"), "tensor", None),
            P(("groups", "store"), None, None),
            P(("groups", "store")),
            P(("groups", "store")),
        ),
        out_specs=P(("groups", "store"), "tensor"),
        check_vma=False,
    )
```

```python
import functools

import jax
import jax.numpy as jnp
from jax import lax
from jax.experimental import pallas as pl
from jax.experimental.pallas import tpu as pltpu
from jax.sharding import PartitionSpec as P

ADAPTER_SCALE = 0.5
MESH = pl.DeviceIdType.MESH
F32 = jnp.float32
BF16 = jnp.bfloat16


def adapter_of_token(lengths_row, ids_row, tokens):
    count = lengths_row.shape[1]
    down = lax.broadcasted_iota(jnp.int32, (count, count), 0)
    across = lax.broadcasted_iota(jnp.int32, (count, count), 1)
    column = jnp.sum(jnp.where(down == across, lengths_row, 0.0), axis=1, keepdims=True)
    ends = jnp.sum(jnp.where(down <= across, column, 0.0), axis=0, keepdims=True)
    starts = ends - lengths_row
    token = lax.broadcasted_iota(jnp.int32, (tokens, count), 0).astype(F32)
    inside = (token >= starts) & (token < ends)
    return jnp.sum(jnp.where(inside, ids_row, 0.0), axis=1, keepdims=True)


def pack(value, rank):
    folded = value + pltpu.roll(value, rank, 1)
    rows = value.shape[0] // 2
    low = lax.broadcasted_iota(jnp.int32, (rows, 2 * rank), 1) < rank
    return jnp.where(low, folded[:rows], folded[rows:]).astype(BF16)


def unpack(value, rank):
    value = value.astype(F32)
    turned = pltpu.roll(value, rank, 1)
    low = lax.broadcasted_iota(jnp.int32, value.shape, 1) < rank
    return jnp.concatenate(
        [jnp.where(low, value, turned), jnp.where(low, turned, value)], axis=0
    )


def kernel(
    n, rank, x_ref, w_ref, down_ref, up_ref, len_ref, ids_ref, out_ref,
    xv, x2c, x2e, xe, wb, big, bigb, upx, meta, metap, metae, tok, toke, acc, acce,
    snd, rcv, snde, rcve, basev, bsend, brecv,
    loc, wsem, ls, lr, bs, br, pair_s, pair_r, us, ur, ss, sr, es, er,
):
    tokens = x_ref.shape[0]
    quarter = x_ref.shape[1] // 2
    lanes = down_ref.shape[0]
    adapters = lanes // rank
    extra = x2e.shape[1]
    common = x2c.shape[1]
    half_out = out_ref.shape[1]
    tile = half_out // 2
    requests = len_ref.shape[1]
    length = n // 2

    s = lax.axis_index("store")
    t = lax.axis_index("tensor")
    p = s // 2
    y = lax.rem(s, 2)
    sibling = {"tensor": 1 - t}
    partner = {"store": 2 * p + 1 - y}
    diagonal = {"store": 2 * p + 1 - y, "tensor": 1 - t}
    right = {"store": s + 2}
    left = {"store": s - 2}
    has_left = p > 0
    has_right = p < length - 1
    is_end = (p == 0) | (p == length - 1)
    is_inner = (p > 0) & (p < length - 1)
    is_helper = (p == 1) | (p == length - 2)
    peer = {"store": s + jnp.where((p == 0) | (p == length - 2), 2, -2)}

    def columns(which, width):
        return pl.ds(pl.multiple_of(which * width, 128), width)

    def common_of(which):
        return pl.ds(pl.multiple_of(which * quarter, 128), common)

    def extra_of(which):
        return pl.ds(pl.multiple_of(which * quarter + common, 128), extra)

    own_rows = pl.ds(0, tokens)
    other_rows = pl.ds(tokens, tokens)
    down_part = (slice(None), pl.ds(0, common))
    up_part = (slice(None), pl.ds(common, tile))

    def local_copy(src, dst, i):
        return pltpu.make_async_copy(src, dst, loc.at[i])

    local_a = local_copy(down_ref.at[:, common_of(y)], big.at[(2 * p,) + down_part], 0)
    local_u = local_copy(up_ref.at[:, columns(t * 2 + y, tile)], big.at[(2 * p,) + up_part], 1)
    local_b = local_copy(down_ref.at[:, extra_of(y)], bigb.at[2 * p], 2)
    local_xe = local_copy(x_ref.at[:, extra_of(y)], x2e.at[own_rows], 3)
    local_xc = local_copy(x_ref.at[:, common_of(y)], x2c.at[own_rows], 4)
    local_x = local_copy(x_ref, xv, 5)

    def weight_copy(j):
        which = lax.rem((1 - t) * 2 + j, 4)
        return pltpu.make_async_copy(
            w_ref.at[:, columns(which, tile)], wb.at[j % 2], wsem.at[j]
        )

    barrier = pltpu.get_barrier_semaphore()
    for who in (sibling, partner, diagonal):
        pl.semaphore_signal(barrier, inc=1, device_id=who, device_id_type=MESH)

    @pl.when(has_left)
    def _():
        pl.semaphore_signal(barrier, inc=1, device_id=left, device_id_type=MESH)

    @pl.when(has_right)
    def _():
        pl.semaphore_signal(barrier, inc=1, device_id=right, device_id_type=MESH)

    for copy in (local_a, local_u, local_b, local_xe, local_xc, local_x):
        copy.start()
    weight_copy(0).start()
    weight_copy(1).start()
    meta[...] = jnp.zeros_like(meta)
    meta[0:1, 0:requests] = len_ref[...]
    meta[1:2, 0:requests] = ids_ref[...]

    def remote(src, dst, send, recv, who):
        return pltpu.make_async_remote_copy(
            src_ref=src, dst_ref=dst, send_sem=send, recv_sem=recv,
            device_id=who, device_id_type=MESH,
        )

    def pair_copy(src, dst, i, who=partner):
        return remote(src, dst, pair_s.at[i], pair_r.at[i], who)

    pair_a = pair_copy(down_ref.at[:, common_of(1 - y)], big.at[(2 * p + 1,) + down_part], 0)
    pair_u = pair_copy(
        up_ref.at[:, columns(t * 2 + 1 - y, tile)], big.at[(2 * p + 1,) + up_part], 1
    )
    pair_meta = pair_copy(meta, metap, 2)
    pair_xe = pair_copy(x_ref.at[:, extra_of(1 - y)], x2e.at[other_rows], 3)
    pair_b = pair_copy(down_ref.at[:, extra_of(1 - y)], bigb.at[2 * p + 1], 4)
    pair_xc = pair_copy(x_ref.at[:, common_of(1 - y)], x2c.at[other_rows], 5)
    base_copy = pair_copy(bsend, brecv, 6, sibling)

    def end_copy(src, dst, i):
        return remote(src, dst, es.at[i], er.at[i], peer)

    end_x = [
        end_copy(x2e.at[own_rows], xe.at[own_rows], 0),
        end_copy(x2e.at[other_rows], xe.at[other_rows], 1),
    ]
    end_meta = [end_copy(meta, metae.at[0], 2), end_copy(metap, metae.at[1], 3)]
    end_sum = end_copy(snde, rcve, 4)

    def position(direction, k):
        return p - k if direction == 0 else p + k

    def inside(direction, k):
        return position(direction, k) >= 0 if direction == 0 else position(direction, k) < length

    def line(buffer, send, recv, direction, k, o):
        slot = buffer.at[2 * position(direction, k) + o]
        return remote(
            slot, slot, send.at[direction, k, o], recv.at[direction, k, o],
            right if direction == 0 else left,
        )

    def arrival(buffer, send, recv, direction, k, o):
        slot = buffer.at[2 * position(direction, k) + o]
        return remote(
            slot, slot, send.at[direction, k - 1, o], recv.at[direction, k - 1, o], partner
        )

    goes = (has_right, has_left)
    goes_b = (p < length - 2, p > 1)

    def send_a(k, o, direction):
        @pl.when(goes[direction])
        def _():
            line(big, ls, lr, direction, k, o).start()

    def send_b(k, o, direction):
        @pl.when(goes_b[direction])
        def _():
            line(bigb, bs, br, direction, k, o).start()

    def forward_up(slot):
        return remote(big.at[(slot,) + up_part], upx.at[slot], us.at[slot], ur.at[slot], partner)

    lane_adapter = (lax.broadcasted_iota(jnp.int32, (1, lanes), 1) // rank).astype(F32)

    def wanted(q, o):
        store = 2 * q + (y if o == 0 else 1 - y)
        return lane_adapter + (store * adapters).astype(F32)

    def product(q, x, buffer, width, adapter):
        weights = buffer[pl.ds(2 * q, 2), :, 0:width].reshape(2 * lanes, width)
        full = lax.dot_general(
            x, weights, (((1,), (1,)), ((), ())), preferred_element_type=F32
        )
        return jnp.where(adapter == wanted(q, 0), full[:, 0:lanes], 0.0) + jnp.where(
            adapter == wanted(q, 1), full[:, lanes:], 0.0
        )

    def project_a(q, first):
        rows = slice(first, first + tokens)
        acc[rows, :] += product(q, x2c[rows, :], big, common, tok[rows, :])

    def project_b(q, first):
        rows = slice(first, first + tokens)
        acc[rows, :] += product(q, x2e[rows, :], bigb, extra, tok[rows, :])

    def token_rows(ref, dst, first):
        lengths_row = ref[0:1, 0:requests].astype(F32)
        ids_row = ref[1:2, 0:requests].astype(F32)
        dst[first:first + tokens, :] = jnp.broadcast_to(
            adapter_of_token(lengths_row, ids_row, tokens), (tokens, lanes)
        )

    count = 3 + has_left.astype(jnp.int32) + has_right.astype(jnp.int32)
    pl.semaphore_wait(barrier, count)
    pair_a.start()
    pair_u.start()
    pair_meta.start()
    local_a.wait()
    local_u.wait()
    for direction in (0, 1):
        send_a(0, 0, direction)
    forward_up(2 * p).start()
    acc[...] = jnp.zeros_like(acc)
    token_rows(meta, tok, 0)
    local_b.wait()
    local_xe.wait()
    local_xc.wait()
    pair_a.wait_recv()
    pair_u.wait_recv()
    for direction in (0, 1):
        send_a(0, 1, direction)
    forward_up(2 * p + 1).start()
    pair_a.wait_send()
    pair_u.wait_send()
    pair_b.start()
    pair_xe.start()
    project_a(p, 0)

    local_x.wait()
    for j in range(4):
        weight_copy(j).wait()
        part = jnp.dot(xv[...], wb[j % 2], preferred_element_type=F32)
        at = (j % 2) * tile
        if j < 2:
            bsend[:, at:at + tile] = part.astype(BF16)
            weight_copy(j + 2).start()
        else:
            basev[:, at:at + tile] = part
        if j == 1:
            base_copy.start()

    def step_a(k):
        for o in (0, 1):
            for direction in (0, 1):
                @pl.when(inside(direction, k))
                def _():
                    arrival(big, ls, lr, direction, k, o).wait_recv()
                    send_a(k, o, direction)
                    forward_up(2 * position(direction, k) + o).start()

        for direction in (0, 1):
            @pl.when(inside(direction, k))
            def _():
                project_a(position(direction, k), 0)

    @pl.when(is_end)
    def _():
        end_meta[0].start()
        end_x[0].start()

    step_a(1)
    pair_b.wait_recv()
    for o in (0, 1):
        for direction in (0, 1):
            send_b(0, o, direction)

    pair_xe.wait_send()
    pair_xc.start()
    pair_meta.wait_recv()
    token_rows(metap, tok, tokens)
    base_copy.wait_recv()
    basev[...] += brecv[...].astype(F32)
    pair_xe.wait_recv()

    @pl.when(is_end)
    def _():
        end_meta[1].start()
        end_x[1].start()

    def loop_a(k, carry):
        step_a(k)
        return carry

    lax.fori_loop(2, length, loop_a, 0)

    @pl.when(is_inner)
    def _():
        project_b(p, 0)

        def loop_b(k, carry):
            for o in (0, 1):
                for direction in (0, 1):
                    @pl.when(inside(direction, k))
                    def _():
                        arrival(bigb, bs, br, direction, k, o).wait_recv()
                        send_b(k, o, direction)

            for direction in (0, 1):
                @pl.when(inside(direction, k))
                def _():
                    project_b(position(direction, k), 0)

            return carry

        lax.fori_loop(1, length - 1, loop_b, 0)

    @pl.when(is_helper)
    def _():
        for copy in end_meta + end_x:
            copy.wait_recv()
        for i in (0, 1):
            token_rows(metae.at[i], toke, i * tokens)
        acce[...] = jnp.zeros_like(acce)

        def loop_e(q, carry):
            acce[...] += product(q, xe[...], bigb, extra, toke[...])
            return carry

        lax.fori_loop(0, length, loop_e, 0)
        for i in (0, 1):
            snde[i] = pack(acce[i * tokens:(i + 1) * tokens, :], rank)
        end_sum.start()

    pair_xc.wait_recv()

    def loop_partner(q, carry):
        project_a(q, tokens)

        @pl.when(is_inner)
        def _():
            project_b(q, tokens)

        return carry

    lax.fori_loop(0, length, loop_partner, 0)

    @pl.when(is_end)
    def _():
        end_sum.wait_recv()
        for i in (0, 1):
            rows = slice(i * tokens, (i + 1) * tokens)
            parity = tok[rows, :] - 2.0 * jnp.floor(tok[rows, :] * 0.5)
            acc[rows, :] += jnp.where(parity == lane_adapter, unpack(rcve[i], rank), 0.0)

    snd[1] = pack(acc[tokens:, :], rank)
    snd[0] = pack(acc[0:tokens, :], rank)
    sums = [
        remote(snd.at[1], rcv.at[2], ss.at[2], sr.at[2], diagonal),
        remote(snd.at[1], rcv.at[1], ss.at[1], sr.at[1], partner),
        remote(snd.at[0], rcv.at[0], ss.at[0], sr.at[0], sibling),
    ]
    for copy in sums:
        copy.start()

    def wait_up(slot, carry):
        forward_up(slot).wait()
        return carry

    lax.fori_loop(0, n, wait_up, 0)
    for copy in sums:
        copy.wait_recv()
    shrink = acc[0:tokens, :]
    for i in range(3):
        shrink = shrink + unpack(rcv[i], rank)
    own_adapter = tok[0:tokens, :]

    def expand(q, carry):
        parts = [jnp.where(own_adapter == wanted(q, o), shrink, 0.0) for o in (0, 1)]
        rows = jnp.concatenate(parts, axis=1).astype(BF16)
        mine = big[pl.ds(2 * q, 2), :, common:common + tile].reshape(2 * lanes, tile)
        theirs = jnp.concatenate([upx[2 * q + 1], upx[2 * q]], axis=0)
        a, b = carry
        a = a + jnp.dot(rows, mine, preferred_element_type=F32)
        b = b + jnp.dot(rows, theirs, preferred_element_type=F32)
        return a, b

    zero = jnp.zeros((tokens, tile), F32)
    a, b = lax.fori_loop(0, length, expand, (zero, zero))
    for which, value in ((y, a), (1 - y, b)):
        at = columns(which, tile)
        total = basev[:, at] + ADAPTER_SCALE * value.astype(BF16).astype(F32)
        out_ref[:, at] = total.astype(BF16)

    def drain(k, carry):
        for o in (0, 1):
            for direction in (0, 1):
                @pl.when(goes[direction] & inside(direction, k))
                def _():
                    line(big, ls, lr, direction, k, o).wait_send()

                @pl.when(goes_b[direction] & inside(direction, k))
                def _():
                    line(bigb, bs, br, direction, k, o).wait_send()

        return carry

    lax.fori_loop(0, length - 1, drain, 0)

    @pl.when(is_end)
    def _():
        for copy in end_meta + end_x:
            copy.wait_send()

    @pl.when(is_helper)
    def _():
        end_sum.wait_send()

    for copy in [pair_meta, pair_b, pair_xc, base_copy] + sums:
        copy.wait_send()


def local(hidden_in, base_weight, adapter_down, adapter_up, lengths, adapter_ids):
    n = lax.axis_size("store")
    tokens, depth = hidden_in.shape
    quarter = depth // 2
    adapters, _, rank = adapter_down.shape
    lanes = adapters * rank
    width = adapter_up.shape[2]
    half = width // 2
    tile = half // 2
    length = n // 2
    assert length >= 4 and adapters == 2
    extra = quarter * 5 // 16 // 128 * 128
    common = quarter - extra
    requests = lengths.shape[0]
    dma = pltpu.SemaphoreType.DMA
    vmem = pl.BlockSpec(memory_space=pltpu.VMEM)
    hbm = pl.BlockSpec(memory_space=pl.ANY)
    return pl.pallas_call(
        functools.partial(kernel, n, rank),
        out_shape=jax.ShapeDtypeStruct((tokens, half), BF16),
        in_specs=[hbm, hbm, hbm, hbm, vmem, vmem],
        out_specs=vmem,
        scratch_shapes=[
            pltpu.VMEM((tokens, depth), BF16),
            pltpu.VMEM((2 * tokens, common), BF16),
            pltpu.VMEM((2 * tokens, extra), BF16),
            pltpu.VMEM((2 * tokens, extra), BF16),
            pltpu.VMEM((2, depth, tile), BF16),
            pltpu.VMEM((n, lanes, common + tile), BF16),
            pltpu.VMEM((n, lanes, extra), BF16),
            pltpu.VMEM((n, lanes, tile), BF16),
            pltpu.VMEM((8, 128), jnp.int32),
            pltpu.VMEM((8, 128), jnp.int32),
            pltpu.VMEM((2, 8, 128), jnp.int32),
            pltpu.VMEM((2 * tokens, lanes), F32),
            pltpu.VMEM((2 * tokens, lanes), F32),
            pltpu.VMEM((2 * tokens, lanes), F32),
            pltpu.VMEM((2 * tokens, lanes), F32),
            pltpu.VMEM((2, tokens // 2, lanes), BF16),
            pltpu.VMEM((3, tokens // 2, lanes), BF16),
            pltpu.VMEM((2, tokens // 2, lanes), BF16),
            pltpu.VMEM((2, tokens // 2, lanes), BF16),
            pltpu.VMEM((tokens, half), F32),
            pltpu.VMEM((tokens, half), BF16),
            pltpu.VMEM((tokens, half), BF16),
            dma((6,)),
            dma((4,)),
            dma((2, length, 2)),
            dma((2, length, 2)),
            dma((2, length, 2)),
            dma((2, length, 2)),
            dma((7,)),
            dma((7,)),
            dma((n,)),
            dma((n,)),
            dma((3,)),
            dma((3,)),
            dma((5,)),
            dma((5,)),
        ],
        compiler_params=pltpu.CompilerParams(
            collective_id=0, has_side_effects=True, vmem_limit_bytes=62 * 1024 * 1024
        ),
    )(
        hidden_in, base_weight,
        adapter_down.transpose(0, 2, 1).reshape(lanes, depth),
        adapter_up.reshape(lanes, width),
        lengths.reshape(1, requests), adapter_ids.reshape(1, requests),
    )


def solution(mesh):
    return jax.shard_map(
        local,
        mesh=mesh,
        in_specs=(
            P(("groups", "store"), "tensor"),
            P("tensor", None),
            P(("groups", "store"), "tensor", None),
            P(("groups", "store"), None, None),
            P(("groups", "store")),
            P(("groups", "store")),
        ),
        out_specs=P(("groups", "store"), "tensor"),
        check_vma=False,
    )
```
